32 devices in a mesh: span: 4 (over y, x), seq: 8 (over z, core).
Axes of the slice: x: 2, y: 2, z: 4, core: 2. Of those that a mesh axis runs over, the one named last changes fastest.
Arguments:
- hidden_in: bfloat16 [1024, 6144], P(('span', 'seq')), may hold values from -6 to 6
- qkv_weight: bfloat16 [6144, 3, 4096], P(None, None, 'seq'), may hold values from -0.078125 to 0.078125
- out_weight: bfloat16 [4096, 6144], P('seq'), may hold values from -0.09375 to 0.09375
- mod_table: bfloat16 [16, 2, 6144], replicated, may hold values from -1.5 to 9
- noise_level: int32 [4], replicated, may hold values from 0 to 15
- range_lo: int32 [4, 4], replicated, may hold values from 0 to 127
- range_len: int32 [4, 4], replicated, may hold values from 1 to 128
Outputs:
- hidden_out: bfloat16 [1024, 6144], P(('span', 'seq'))
The draws below stay inside these ranges and needn't reach their ends.
Inputs may be any that keep to these rules, and one draw needn't show every extreme that they name: Only entries whose key span comes before the query span are read; range_lo + range_len stays below 256.
All inputs are finite; a program needn't handle non-finite values.
Results may differ from the reference program's by a relative error of at most 0.015.
The reference program's roundings to bfloat16 on the way (of `normed`, `projected`, `weights` and `attended`) count: a program that leaves them out, or rounds other values in their place, can miss the bound.
Values may be sent and summed in bfloat16 or wider, within the bound.
A program may use at most 128 MiB of HBM per device.

```python
import jax
import jax.numpy as jnp
from jax import lax

D = 6144
HEADS = 32
HD = 128
LEVELS = 16
SPAN_TOK = 256
SPANS = 4
TOKENS = 1024
N_SEQ = 8


def draw_mod_table(key, part):
    key = jax.random.fold_in(key, 7)
    gain_key, shift_key = jax.random.split(key)
    shifts = jnp.clip(0.3 * jax.random.normal(shift_key, (LEVELS, 1, D), jnp.float32), -1.5, 1.5)
    gains = jnp.clip(0.5 * jax.random.normal(gain_key, (LEVELS, 1, D), jnp.float32), -1.5, 1.5)
    return jnp.concatenate((gains, shifts), axis=1).astype(jnp.bfloat16)


def set_ends(entries, key, least, largest):
    longest = entries.shape.index(max(entries.shape))
    spots = []
    for shift in (0, 1):
        where = [jax.random.randint(jax.random.fold_in(key, axis), (), 0, length) for axis, length in enumerate(entries.shape)]
        where[longest] = (where[longest] + shift) % entries.shape[longest]
        spots.append(tuple(where))
    return entries.at[spots[0]].set(least).at[spots[1]].set(largest)


def steps_of(own_key, dims, cuts, smallest, largest):
    def one(axis_at, parts):
        heights = jax.random.uniform(jax.random.fold_in(jax.random.fold_in(own_key, 6), axis_at), (parts,), jnp.float32, smallest / len(cuts), largest / len(cuts))
        return jnp.repeat(jnp.exp(heights), dims[axis_at] // parts).reshape((-1,) + (1,) * (len(dims) - axis_at - 1))

    level = one(*cuts[0])
    for cut in cuts[1:]:
        level = level * one(*cut)
    return level


def gaussian(key, shape, scale, most, cuts=(), kind=jnp.bfloat16):
    values = jax.random.normal(key, shape, jnp.float32) * scale
    if len(cuts) > 0:
        values = steps_of(key, shape, cuts, -0.22, 0.18) * values
    return jnp.clip(values, min=-most, max=most).astype(kind)


def setup_inputs(seed: int = 0) -> dict:
    seeds = jax.random.split(jax.random.key(seed), 8)
    return {
        "hidden_in": gaussian(seeds[0], (TOKENS, D), 1.0, 6.0, ((0, 32),)),
        "qkv_weight": gaussian(seeds[1], (D, 3, HEADS * HD), D ** -0.5, 0.078125, ((2, 8),)),
        "out_weight": gaussian(seeds[2], (HEADS * HD, D), (HEADS * HD) ** -0.5, 0.09375, ((0, 8),)),
        "mod_table": draw_mod_table(jax.random.fold_in(seeds[7], 71), 0),
        "noise_level": set_ends(jax.random.randint(seeds[4], (SPANS,), 0, LEVELS), jax.random.fold_in(seeds[4], 1), 0, LEVELS - 1).astype(jnp.int32),
        "range_lo": set_ends(jax.random.randint(seeds[5], (SPANS, SPANS), 0, SPAN_TOK // 2), jax.random.fold_in(seeds[5], 1), 0, (SPAN_TOK // 2) - 1).astype(jnp.int32),
        "range_len": set_ends(jax.random.randint(seeds[6], (SPANS, SPANS), 1, SPAN_TOK // 2 + 1), jax.random.fold_in(seeds[6], 1), 1, (SPAN_TOK // 2 + 1) - 1).astype(jnp.int32),
    }


def reference(hidden_in, qkv_weight, out_weight, mod_table, noise_level, range_lo, range_len):
    width_all = HEADS * HD
    xfloat = hidden_in.astype(jnp.float32).reshape(SPANS, SPAN_TOK, D)
    modulation = jnp.take(mod_table.astype(jnp.float32), noise_level, axis=0)
    row_mean = lax.optimization_barrier(jnp.mean(xfloat, axis=-1, keepdims=True))
    row_var = lax.optimization_barrier(jnp.mean((xfloat - row_mean) ** 2, axis=-1, keepdims=True))
    normed = (xfloat - row_mean) * lax.rsqrt(row_var + 1e-06) * (1.0 + modulation[:, 0:1]) + modulation[:, 1:2]
    normed = normed.astype(jnp.bfloat16).reshape(TOKENS, D)
    projected = jnp.dot(normed, qkv_weight.reshape(D, 3 * width_all), preferred_element_type=jnp.float32).astype(jnp.bfloat16)
    queries = projected[:, :width_all].reshape(TOKENS, HEADS, HD).transpose(1, 0, 2)
    keys_all = projected[:, width_all:2 * width_all].reshape(TOKENS, HEADS, HD).transpose(1, 0, 2)
    values_all = projected[:, 2 * width_all:].reshape(TOKENS, HEADS, HD).transpose(1, 0, 2)
    positions = jnp.arange(TOKENS, dtype=jnp.int32)
    key_span = positions // SPAN_TOK
    offset = positions - key_span * SPAN_TOK
    scale = HD ** (-0.5)

    def attend_span(span_index):
        lo_key = jnp.take(range_lo[span_index], key_span)
        len_key = jnp.take(range_len[span_index], key_span)
        visible = (key_span == span_index) | (key_span < span_index) & (offset >= lo_key) & (offset < lo_key + len_key)

        def attend_head(head_index):
            query_rows = lax.dynamic_slice_in_dim(queries[head_index], (span_index * SPAN_TOK).astype(jnp.int32), SPAN_TOK, 0)
            scores = jnp.dot(query_rows, keys_all[head_index].T, preferred_element_type=jnp.float32) * scale
            masked = jnp.where(visible[None, :], scores, -1e+30)
            row_max = lax.optimization_barrier(jnp.max(masked, axis=-1, keepdims=True))
            weights = jnp.where(visible[None, :], jnp.exp(scores - row_max), 0.0)
            denominator = lax.optimization_barrier(jnp.sum(weights, axis=-1, keepdims=True))
            summed = jnp.dot(weights.astype(jnp.bfloat16), values_all[head_index], preferred_element_type=jnp.float32)
            return summed / denominator
        heads_out = lax.map(attend_head, jnp.arange(HEADS, dtype=jnp.int32))
        return heads_out.transpose(1, 0, 2).reshape(SPAN_TOK, width_all).astype(jnp.bfloat16)
    attended = lax.map(attend_span, jnp.arange(SPANS, dtype=jnp.int32)).reshape(TOKENS, width_all)
    group_width = width_all // N_SEQ
    attended_groups = attended.reshape(TOKENS, N_SEQ, group_width).transpose(1, 0, 2)
    weight_groups = out_weight.reshape(N_SEQ, group_width, D)

    def add_group(running, group_pair):
        rows_here, weight_here = group_pair
        term = jnp.dot(rows_here, weight_here, preferred_element_type=jnp.float32).astype(jnp.bfloat16)
        term = lax.optimization_barrier(term)
        return (running + term.astype(jnp.float32), None)
    summed, _ = lax.scan(add_group, jnp.zeros((TOKENS, D), jnp.float32), (attended_groups, weight_groups))
    return (hidden_in.astype(jnp.float32) + summed).astype(jnp.bfloat16)
```

```python
import functools

import jax
import jax.numpy as jnp
from jax import lax
from jax.experimental import pallas as pl
from jax.experimental.pallas import tpu as pltpu
from jax.sharding import PartitionSpec as P

HD = 128
F32 = jnp.float32
BF16 = jnp.bfloat16
MESH = pl.DeviceIdType.MESH


def kernel(
    nspan, nseq,
    level_ref, lo_ref, len_ref, x_ref, mod_ref, w_hbm, wo_hbm, out_ref,
    w, wo, xg, proj, win_out, win_in, att, acc, mx, den, term, sib, from_low, from_high, fwd, total,
    w_sem, wo_sem,
    g_send_up, g_send_down, g_send_sib, g_recv_z, g_recv_sib,
    k_send, k_recv,
    s_send_z, s_send_sib, s_recv_low, s_recv_high, s_recv_sib,
):
    span = lax.axis_index("span")
    seq = lax.axis_index("seq")
    nz = nseq // 2
    z = seq // 2
    core = seq - 2 * z
    rows, width = x_ref.shape
    tok = rows * nseq
    chunk = 2 * rows
    wdev = w.shape[2]
    heads = wdev // HD
    half = tok // 2
    up, down, other = seq + 2, seq - 2, 2 * z + 1 - core
    has_up, has_down = z < nz - 1, z > 0

    loads = [pltpu.make_async_copy(w_hbm.at[p], w.at[p], w_sem.at[p]) for p in range(3)]
    for p in (1, 2, 0):
        loads[p].start()
    load_out = pltpu.make_async_copy(wo_hbm, wo, wo_sem)
    load_out.start()

    barrier = pltpu.get_barrier_semaphore()

    @pl.when(has_up)
    def _():
        pl.semaphore_signal(barrier, inc=1, device_id=(span, up), device_id_type=MESH)

    @pl.when(has_down)
    def _():
        pl.semaphore_signal(barrier, inc=1, device_id=(span, down), device_id_type=MESH)

    pl.semaphore_signal(barrier, inc=1, device_id=(span, other), device_id_type=MESH)

    def greet(i, carry):
        pl.semaphore_signal(
            barrier, inc=1, device_id=(lax.rem(span + i, nspan), seq), device_id_type=MESH
        )
        return carry

    lax.fori_loop(1, nspan, greet, 0)

    def block(index):
        return pl.ds(pl.multiple_of(index * rows, rows), rows)

    def chunk_rows(index):
        return pl.ds(pl.multiple_of(index * chunk, chunk), chunk)

    x = x_ref[...].astype(F32)
    mod = mod_ref[level_ref[span]].astype(F32)
    mean = jnp.mean(x, axis=-1, keepdims=True)
    centred = x - mean
    var = jnp.mean(centred * centred, axis=-1, keepdims=True)
    normed = centred * lax.rsqrt(var + 1e-06) * (1.0 + mod[0:1]) + mod[1:2]
    xg[block(seq), :] = normed.astype(BF16)

    pl.semaphore_wait(
        barrier, has_up.astype(jnp.int32) + has_down.astype(jnp.int32) + nspan
    )

    def g_copy(origin, target, send_sem, recv_sem):
        return pltpu.make_async_remote_copy(
            src_ref=xg.at[block(origin)], dst_ref=xg.at[block(origin)],
            send_sem=send_sem, recv_sem=recv_sem, device_id=(span, target), device_id_type=MESH,
        )

    def g_up(oz):
        return g_copy(2 * oz + core, up, g_send_up.at[oz], g_recv_z.at[oz])

    def g_down(oz):
        return g_copy(2 * oz + core, down, g_send_down.at[oz], g_recv_z.at[oz])

    def g_sib(oz):
        return g_copy(2 * oz + core, other, g_send_sib.at[oz], g_recv_sib.at[oz])

    def g_sib_in(oz):
        return g_copy(2 * oz + 1 - core, other, g_send_sib.at[oz], g_recv_sib.at[oz])

    def gather_step(k, carry):
        low, high = z - k, z + k

        @pl.when((k > 0) & (low >= 0))
        def _():
            g_up(low).wait_recv()

        @pl.when((low >= 0) & has_up)
        def _():
            g_up(low).start()

        @pl.when((k > 0) & (high < nz))
        def _():
            g_down(high).wait_recv()

        @pl.when((high < nz) & has_down)
        def _():
            g_down(high).start()

        @pl.when(low >= 0)
        def _():
            g_sib(low).start()

        @pl.when((k > 0) & (high < nz))
        def _():
            g_sib(high).start()

        @pl.when(k == 0)
        def _():
            for p in range(3):
                loads[p].wait()

        def side(i, c):
            oz = jnp.where(i == 0, low, high)

            @pl.when(((i == 0) & (low >= 0)) | ((i == 1) & (k > 0) & (high < nz)))
            def _():
                g_sib_in(oz).wait_recv()

                def part(p, cc):
                    proj[p, chunk_rows(oz), :] = jnp.dot(
                        xg[chunk_rows(oz), :], w[p], preferred_element_type=F32
                    ).astype(BF16)
                    return cc

                lax.fori_loop(0, 3, part, 0)

            return c

        lax.fori_loop(0, 2, side, 0)
        return carry

    lax.fori_loop(0, nz, gather_step, 0)

    def k_copy(i):
        return pltpu.make_async_remote_copy(
            src_ref=win_out.at[i], dst_ref=win_in.at[span],
            send_sem=k_send.at[i], recv_sem=k_recv.at[span],
            device_id=(i, seq), device_id_type=MESH,
        )

    def k_copy_in(i):
        return pltpu.make_async_remote_copy(
            src_ref=win_out.at[i], dst_ref=win_in.at[i],
            send_sem=k_send.at[i], recv_sem=k_recv.at[i],
            device_id=(i, seq), device_id_type=MESH,
        )

    def send_window(i, carry):
        first = lo_ref[i, span]
        row = lax.broadcasted_iota(jnp.int32, (half, tok), 0)
        col = lax.broadcasted_iota(jnp.int32, (half, tok), 1)
        pick = jnp.where(col == row + first, 1.0, 0.0).astype(BF16)
        for p in range(2):
            win_out[i, p] = jnp.dot(pick, proj[p + 1], preferred_element_type=F32).astype(BF16)
        k_copy(i).start()
        return carry

    lax.fori_loop(span + 1, nspan, send_window, 0)

    scale = HD ** (-0.5)
    trans = (((1,), (1,)), ((), ()))
    for h in range(heads):
        cols = slice(h * HD, (h + 1) * HD)
        s = lax.dot_general(
            proj[0, :, cols], proj[1, :, cols], trans, preferred_element_type=F32
        ) * scale
        m = jnp.max(s, axis=-1, keepdims=True)
        e = jnp.exp(s - m)
        mx[h] = jnp.broadcast_to(m, (tok, HD))
        den[h] = jnp.broadcast_to(jnp.sum(e, axis=-1, keepdims=True), (tok, HD))
        acc[h] = jnp.dot(e.astype(BF16), proj[2, :, cols], preferred_element_type=F32)

    def see_window(j, carry):
        k_copy_in(j).wait_recv()
        seen = lax.broadcasted_iota(jnp.int32, (tok, half), 1) < len_ref[span, j]
        for h in range(heads):
            cols = slice(h * HD, (h + 1) * HD)
            s = lax.dot_general(
                proj[0, :, cols], win_in[j, 0, :, cols], trans, preferred_element_type=F32
            ) * scale
            s = jnp.where(seen, s, -1e30)
            old = mx[h]
            new = jnp.maximum(old, jnp.max(s, axis=-1, keepdims=True))
            e = jnp.where(seen, jnp.exp(s - new[:, 0:1]), 0.0)
            factor = jnp.exp(old - new)
            mx[h] = new
            den[h] = den[h] * factor + jnp.sum(e, axis=-1, keepdims=True)
            acc[h] = acc[h] * factor + jnp.dot(
                e.astype(BF16), win_in[j, 1, :, cols], preferred_element_type=F32
            )
        return carry

    lax.fori_loop(0, span, see_window, 0)
    for h in range(heads):
        att[:, h * HD:(h + 1) * HD] = (acc[h] / den[h]).astype(BF16)

    load_out.wait()

    def s_sib(d):
        return pltpu.make_async_remote_copy(
            src_ref=term.at[block(2 * d + 1 - core)], dst_ref=sib.at[d],
            send_sem=s_send_sib.at[d], recv_sem=s_recv_sib.at[d],
            device_id=(span, other), device_id_type=MESH,
        )

    def project(i, carry):
        d = jnp.where(z >= nz // 2, i, nz - 1 - i)
        term[chunk_rows(d), :] = jnp.dot(
            att[chunk_rows(d), :], wo[...], preferred_element_type=F32
        ).astype(BF16)
        s_sib(d).start()
        return carry

    lax.fori_loop(0, nz, project, 0)

    def s_up(d):
        return pltpu.make_async_remote_copy(
            src_ref=fwd.at[d], dst_ref=from_low.at[d],
            send_sem=s_send_z.at[d], recv_sem=s_recv_low.at[d],
            device_id=(span, up), device_id_type=MESH,
        )

    def s_down(d):
        return pltpu.make_async_remote_copy(
            src_ref=fwd.at[d], dst_ref=from_high.at[d],
            send_sem=s_send_z.at[d], recv_sem=s_recv_high.at[d],
            device_id=(span, down), device_id_type=MESH,
        )

    def pair(d):
        return term[block(2 * d + core), :].astype(F32) + sib[d].astype(F32)

    def scatter_step(t, carry):
        i = t - z
        d_up = nz - 1 - i

        @pl.when((i >= 0) & (d_up > z))
        def _():
            s_sib(d_up).wait_recv()

            @pl.when(has_down)
            def _():
                s_up(d_up).wait_recv()
                fwd[d_up] = (pair(d_up) + from_low[d_up].astype(F32)).astype(BF16)

            @pl.when(jnp.logical_not(has_down))
            def _():
                fwd[d_up] = pair(d_up).astype(BF16)

            s_up(d_up).start()

        d_down = t - (nz - 1 - z)

        @pl.when((d_down >= 0) & (d_down < z))
        def _():
            s_sib(d_down).wait_recv()

            @pl.when(has_up)
            def _():
                s_down(d_down).wait_recv()
                fwd[d_down] = (pair(d_down) + from_high[d_down].astype(F32)).astype(BF16)

            @pl.when(jnp.logical_not(has_up))
            def _():
                fwd[d_down] = pair(d_down).astype(BF16)

            s_down(d_down).start()

        return carry

    lax.fori_loop(0, nz - 1, scatter_step, 0)

    s_sib(z).wait_recv()
    total[...] = x_ref[...].astype(F32) + pair(z)

    @pl.when(has_down)
    def _():
        s_up(z).wait_recv()
        total[...] += from_low[z].astype(F32)

    @pl.when(has_up)
    def _():
        s_down(z).wait_recv()
        total[...] += from_high[z].astype(F32)

    out_ref[...] = total[...].astype(BF16)

    def drain(oz, carry):
        g_sib(oz).wait_send()
        s_sib(oz).wait_send()

        @pl.when((oz <= z) & has_up)
        def _():
            g_up(oz).wait_send()

        @pl.when((oz >= z) & has_down)
        def _():
            g_down(oz).wait_send()

        @pl.when(oz > z)
        def _():
            s_up(oz).wait_send()

        @pl.when(oz < z)
        def _():
            s_down(oz).wait_send()

        return carry

    lax.fori_loop(0, nz, drain, 0)

    def drain_window(i, carry):
        k_copy(i).wait_send()
        return carry

    lax.fori_loop(span + 1, nspan, drain_window, 0)


def local(nspan, nseq, hidden_in, qkv_weight, out_weight, mod_table, noise_level, range_lo, range_len):
    rows, width = hidden_in.shape
    wdev = qkv_weight.shape[2]
    tok = rows * nseq
    nz = nseq // 2
    heads = wdev // HD
    smem = pl.BlockSpec(memory_space=pltpu.SMEM)
    vmem = pl.BlockSpec(memory_space=pltpu.VMEM)
    hbm = pl.BlockSpec(memory_space=pl.ANY)
    dma = pltpu.SemaphoreType.DMA
    return pl.pallas_call(
        functools.partial(kernel, nspan, nseq),
        out_shape=jax.ShapeDtypeStruct((rows, width), BF16),
        in_specs=[smem, smem, smem, vmem, vmem, hbm, hbm],
        out_specs=vmem,
        scratch_shapes=[
            pltpu.VMEM((3, width, wdev), BF16),
            pltpu.VMEM((wdev, width), BF16),
            pltpu.VMEM((tok, width), BF16),
            pltpu.VMEM((3, tok, wdev), BF16),
            pltpu.VMEM((nspan, 2, tok // 2, wdev), BF16),
            pltpu.VMEM((nspan, 2, tok // 2, wdev), BF16),
            pltpu.VMEM((tok, wdev), BF16),
            pltpu.VMEM((heads, tok, HD), F32),
            pltpu.VMEM((heads, tok, HD), F32),
            pltpu.VMEM((heads, tok, HD), F32),
            pltpu.VMEM((tok, width), BF16),
            pltpu.VMEM((nz, rows, width), BF16),
            pltpu.VMEM((nz, rows, width), BF16),
            pltpu.VMEM((nz, rows, width), BF16),
            pltpu.VMEM((nz, rows, width), BF16),
            pltpu.VMEM((rows, width), F32),
            dma((3,)), dma(()),
            dma((nz,)), dma((nz,)), dma((nz,)), dma((nz,)), dma((nz,)),
            dma((nspan,)), dma((nspan,)),
            dma((nz,)), dma((nz,)), dma((nz,)), dma((nz,)), dma((nz,)),
        ],
        compiler_params=pltpu.CompilerParams(
            collective_id=0, has_side_effects=True, vmem_limit_bytes=58 * 1024 * 1024
        ),
    )(
        noise_level, range_lo, range_len, hidden_in, mod_table,
        qkv_weight.transpose(1, 0, 2), out_weight,
    )


def solution(mesh):
    return jax.shard_map(
        functools.partial(local, mesh.shape["span"], mesh.shape["seq"]),
        mesh=mesh,
        in_specs=(
            P(("span", "seq"), None),
            P(None, None, "seq"),
            P("seq", None),
            P(),
            P(),
            P(),
            P(),
        ),
        out_specs=P(("span", "seq"), None),
        check_vma=False,
    )
```

```python
import functools

import jax
import jax.numpy as jnp
from jax import lax
from jax.experimental import pallas as pl
from jax.experimental.pallas import tpu as pltpu
from jax.sharding import PartitionSpec as P

HD = 128
F32 = jnp.float32
BF16 = jnp.bfloat16
MESH = pl.DeviceIdType.MESH


def kernel(
    nspan, nseq,
    level_ref, lo_ref, len_ref, x_ref, mod_ref, w_hbm, wo_hbm, out_ref,
    w, wo, xg, proj, win_out, win_in, att, acc, mx, den, term, sib, from_low, from_high, fwd, total,
    w_sem, wo_sem,
    g_send_up, g_send_down, g_send_sib, g_recv_z, g_recv_sib,
    k_send, k_recv,
    s_send_z, s_send_sib, s_recv_low, s_recv_high, s_recv_sib,
):
    span = lax.axis_index("span")
    seq = lax.axis_index("seq")
    nz = nseq // 2
    z = seq // 2
    core = seq - 2 * z
    rows, width = x_ref.shape
    tok = rows * nseq
    chunk = 2 * rows
    wdev = w.shape[2]
    heads = wdev // HD
    half = tok // 2
    up, down, other = seq + 2, seq - 2, 2 * z + 1 - core
    has_up, has_down = z < nz - 1, z > 0

    loads = [pltpu.make_async_copy(w_hbm.at[p], w.at[p], w_sem.at[p]) for p in range(3)]
    for p in (1, 2, 0):
        loads[p].start()
    load_out = pltpu.make_async_copy(wo_hbm, wo, wo_sem)
    load_out.start()

    barrier = pltpu.get_barrier_semaphore()

    @pl.when(has_up)
    def _():
        pl.semaphore_signal(barrier, inc=1, device_id=(span, up), device_id_type=MESH)

    @pl.when(has_down)
    def _():
        pl.semaphore_signal(barrier, inc=1, device_id=(span, down), device_id_type=MESH)

    pl.semaphore_signal(barrier, inc=1, device_id=(span, other), device_id_type=MESH)

    def greet(i, carry):
        pl.semaphore_signal(
            barrier, inc=1, device_id=(lax.rem(span + i, nspan), seq), device_id_type=MESH
        )
        return carry

    lax.fori_loop(1, nspan, greet, 0)

    def block(index):
        return pl.ds(pl.multiple_of(index * rows, rows), rows)

    def chunk_rows(index):
        return pl.ds(pl.multiple_of(index * chunk, chunk), chunk)

    x = x_ref[...].astype(F32)
    mod = mod_ref[level_ref[span]].astype(F32)
    mean = jnp.mean(x, axis=-1, keepdims=True)
    centred = x - mean
    var = jnp.mean(centred * centred, axis=-1, keepdims=True)
    normed = centred * lax.rsqrt(var + 1e-06) * (1.0 + mod[0:1]) + mod[1:2]
    xg[block(seq), :] = normed.astype(BF16)

    pl.semaphore_wait(
        barrier, has_up.astype(jnp.int32) + has_down.astype(jnp.int32) + nspan
    )

    def columns(part):
        return slice(part * (width // 2), (part + 1) * (width // 2))

    def g_copy(origin, part, target, send_sem, recv_sem):
        return pltpu.make_async_remote_copy(
            src_ref=xg.at[block(origin), columns(part)], dst_ref=xg.at[block(origin), columns(part)],
            send_sem=send_sem, recv_sem=recv_sem, device_id=(span, target), device_id_type=MESH,
        )

    def g_up(oz, part):
        at = 2 * oz + part
        return g_copy(2 * oz + core, part, up, g_send_up.at[at], g_recv_z.at[at])

    def g_down(oz, part):
        at = 2 * oz + part
        return g_copy(2 * oz + core, part, down, g_send_down.at[at], g_recv_z.at[at])

    def g_sib(oz, part):
        at = 2 * oz + part
        return g_copy(2 * oz + core, part, other, g_send_sib.at[at], g_recv_sib.at[at])

    def g_sib_in(oz, part):
        at = 2 * oz + part
        return g_copy(2 * oz + 1 - core, part, other, g_send_sib.at[at], g_recv_sib.at[at])

    def gather_step(k, carry):
        low, high = z - k, z + k

        for half_at in range(2):
            @pl.when((k > 0) & (low >= 0))
            def _():
                g_up(low, half_at).wait_recv()

            @pl.when((low >= 0) & has_up)
            def _():
                g_up(low, half_at).start()

            @pl.when((k > 0) & (high < nz))
            def _():
                g_down(high, half_at).wait_recv()

            @pl.when((high < nz) & has_down)
            def _():
                g_down(high, half_at).start()

            @pl.when(low >= 0)
            def _():
                g_sib(low, half_at).start()

            @pl.when((k > 0) & (high < nz))
            def _():
                g_sib(high, half_at).start()

        @pl.when(k == 0)
        def _():
            for p in range(3):
                loads[p].wait()

        def side(i, c):
            oz = jnp.where(i == 0, low, high)

            @pl.when(((i == 0) & (low >= 0)) | ((i == 1) & (k > 0) & (high < nz)))
            def _():
                g_sib_in(oz, 0).wait_recv()
                g_sib_in(oz, 1).wait_recv()

                def part(p, cc):
                    proj[p, chunk_rows(oz), :] = jnp.dot(
                        xg[chunk_rows(oz), :], w[p], preferred_element_type=F32
                    ).astype(BF16)
                    return cc

                lax.fori_loop(0, 3, part, 0)

            return c

        lax.fori_loop(0, 2, side, 0)
        return carry

    lax.fori_loop(0, nz, gather_step, 0)

    def k_copy(i):
        return pltpu.make_async_remote_copy(
            src_ref=win_out.at[i], dst_ref=win_in.at[span],
            send_sem=k_send.at[i], recv_sem=k_recv.at[span],
            device_id=(i, seq), device_id_type=MESH,
        )

    def k_copy_in(i):
        return pltpu.make_async_remote_copy(
            src_ref=win_out.at[i], dst_ref=win_in.at[i],
            send_sem=k_send.at[i], recv_sem=k_recv.at[i],
            device_id=(i, seq), device_id_type=MESH,
        )

    def send_window(i, carry):
        first = lo_ref[i, span]
        row = lax.broadcasted_iota(jnp.int32, (half, tok), 0)
        col = lax.broadcasted_iota(jnp.int32, (half, tok), 1)
        pick = jnp.where(col == row + first, 1.0, 0.0).astype(BF16)
        for p in range(2):
            win_out[i, p] = jnp.dot(pick, proj[p + 1], preferred_element_type=F32).astype(BF16)
        k_copy(i).start()
        return carry

    lax.fori_loop(span + 1, nspan, send_window, 0)

    scale = HD ** (-0.5)
    trans = (((1,), (1,)), ((), ()))
    for h in range(heads):
        cols = slice(h * HD, (h + 1) * HD)
        s = lax.dot_general(
            proj[0, :, cols], proj[1, :, cols], trans, preferred_element_type=F32
        ) * scale
        m = jnp.max(s, axis=-1, keepdims=True)
        e = jnp.exp(s - m)
        mx[h] = jnp.broadcast_to(m, (tok, HD))
        den[h] = jnp.broadcast_to(jnp.sum(e, axis=-1, keepdims=True), (tok, HD))
        acc[h] = jnp.dot(e.astype(BF16), proj[2, :, cols], preferred_element_type=F32)

    def await_window(j, carry):
        k_copy_in(j).wait_recv()
        return carry

    lax.fori_loop(0, span, await_window, 0)

    load_out.wait()

    def s_sib(d):
        return pltpu.make_async_remote_copy(
            src_ref=term.at[block(2 * d + 1 - core)], dst_ref=sib.at[d],
            send_sem=s_send_sib.at[d], recv_sem=s_recv_sib.at[d],
            device_id=(span, other), device_id_type=MESH,
        )

    def project(d):
        mine = chunk_rows(d)

        def see_window(j, carry):
            seen = lax.broadcasted_iota(jnp.int32, (chunk, half), 1) < len_ref[span, j]
            for h in range(heads):
                cols = slice(h * HD, (h + 1) * HD)
                s = lax.dot_general(
                    proj[0, mine, cols], win_in[j, 0, :, cols], trans,
                    preferred_element_type=F32,
                ) * scale
                s = jnp.where(seen, s, -1e30)
                old = mx[h, mine, :]
                new = jnp.maximum(old, jnp.max(s, axis=-1, keepdims=True))
                e = jnp.where(seen, jnp.exp(s - new[:, 0:1]), 0.0)
                factor = jnp.exp(old - new)
                mx[h, mine, :] = new
                den[h, mine, :] = den[h, mine, :] * factor + jnp.sum(e, axis=-1, keepdims=True)
                acc[h, mine, :] = acc[h, mine, :] * factor + jnp.dot(
                    e.astype(BF16), win_in[j, 1, :, cols], preferred_element_type=F32
                )
            return carry

        lax.fori_loop(0, span, see_window, 0)
        for h in range(heads):
            att[mine, h * HD:(h + 1) * HD] = (acc[h, mine, :] / den[h, mine, :]).astype(BF16)
        term[mine, :] = jnp.dot(
            att[mine, :], wo[...], preferred_element_type=F32
        ).astype(BF16)
        s_sib(d).start()

    def s_up(d, part):
        return pltpu.make_async_remote_copy(
            src_ref=fwd.at[d, :, columns(part)], dst_ref=from_low.at[d, :, columns(part)],
            send_sem=s_send_z.at[2 * d + part], recv_sem=s_recv_low.at[2 * d + part],
            device_id=(span, up), device_id_type=MESH,
        )

    def s_down(d, part):
        return pltpu.make_async_remote_copy(
            src_ref=fwd.at[d, :, columns(part)], dst_ref=from_high.at[d, :, columns(part)],
            send_sem=s_send_z.at[2 * d + part], recv_sem=s_recv_high.at[2 * d + part],
            device_id=(span, down), device_id_type=MESH,
        )

    def pair(d, cols=slice(None)):
        return term[block(2 * d + core), cols].astype(F32) + sib[d, :, cols].astype(F32)

    def pass_on(d, copy, arrived, more):
        s_sib(d).wait_recv()
        for part in range(2):
            cols = columns(part)

            @pl.when(more)
            def _():
                copy(d, part).wait_recv()
                fwd[d, :, cols] = (pair(d, cols) + arrived[d, :, cols].astype(F32)).astype(BF16)

            @pl.when(jnp.logical_not(more))
            def _():
                fwd[d, :, cols] = pair(d, cols).astype(BF16)

            copy(d, part).start()

    def scatter_step(t):
        i = t - z
        d_up = nz - 1 - i

        @pl.when((i >= 0) & (d_up > z))
        def _():
            pass_on(d_up, s_up, from_low, has_down)

        d_down = t - (nz - 1 - z)

        @pl.when((d_down >= 0) & (d_down < z))
        def _():
            pass_on(d_down, s_down, from_high, has_up)

    at_end = jnp.logical_not(has_up & has_down)

    def step(u, carry):
        @pl.when(u < nz)
        def _():
            project(jnp.where(z >= nz // 2, u, nz - 1 - u))

        t = jnp.where(at_end, u, u - nz)

        @pl.when((t >= 0) & (t < nz - 1))
        def _():
            scatter_step(t)

        return carry

    lax.fori_loop(0, 2 * nz - 1, step, 0)

    s_sib(z).wait_recv()
    total[...] = x_ref[...].astype(F32) + pair(z)

    @pl.when(has_down)
    def _():
        s_up(z, 0).wait_recv()
        s_up(z, 1).wait_recv()
        total[...] += from_low[z].astype(F32)

    @pl.when(has_up)
    def _():
        s_down(z, 0).wait_recv()
        s_down(z, 1).wait_recv()
        total[...] += from_high[z].astype(F32)

    out_ref[...] = total[...].astype(BF16)

    def drain(oz, carry):
        s_sib(oz).wait_send()
        for part in range(2):
            g_sib(oz, part).wait_send()

            @pl.when((oz <= z) & has_up)
            def _():
                g_up(oz, part).wait_send()

            @pl.when((oz >= z) & has_down)
            def _():
                g_down(oz, part).wait_send()

            @pl.when(oz > z)
            def _():
                s_up(oz, part).wait_send()

            @pl.when(oz < z)
            def _():
                s_down(oz, part).wait_send()

        return carry

    lax.fori_loop(0, nz, drain, 0)

    def drain_window(i, carry):
        k_copy(i).wait_send()
        return carry

    lax.fori_loop(span + 1, nspan, drain_window, 0)


def local(nspan, nseq, hidden_in, qkv_weight, out_weight, mod_table, noise_level, range_lo, range_len):
    rows, width = hidden_in.shape
    wdev = qkv_weight.shape[2]
    tok = rows * nseq
    nz = nseq // 2
    heads = wdev // HD
    smem = pl.BlockSpec(memory_space=pltpu.SMEM)
    vmem = pl.BlockSpec(memory_space=pltpu.VMEM)
    hbm = pl.BlockSpec(memory_space=pl.ANY)
    dma = pltpu.SemaphoreType.DMA
    return pl.pallas_call(
        functools.partial(kernel, nspan, nseq),
        out_shape=jax.ShapeDtypeStruct((rows, width), BF16),
        in_specs=[smem, smem, smem, vmem, vmem, hbm, hbm],
        out_specs=vmem,
        scratch_shapes=[
            pltpu.VMEM((3, width, wdev), BF16),
            pltpu.VMEM((wdev, width), BF16),
            pltpu.VMEM((tok, width), BF16),
            pltpu.VMEM((3, tok, wdev), BF16),
            pltpu.VMEM((nspan, 2, tok // 2, wdev), BF16),
            pltpu.VMEM((nspan, 2, tok // 2, wdev), BF16),
            pltpu.VMEM((tok, wdev), BF16),
            pltpu.VMEM((heads, tok, HD), F32),
            pltpu.VMEM((heads, tok, HD), F32),
            pltpu.VMEM((heads, tok, HD), F32),
            pltpu.VMEM((tok, width), BF16),
            pltpu.VMEM((nz, rows, width), BF16),
            pltpu.VMEM((nz, rows, width), BF16),
            pltpu.VMEM((nz, rows, width), BF16),
            pltpu.VMEM((nz, rows, width), BF16),
            pltpu.VMEM((rows, width), F32),
            dma((3,)), dma(()),
            dma((2 * nz,)), dma((2 * nz,)), dma((2 * nz,)), dma((2 * nz,)), dma((2 * nz,)),
            dma((nspan,)), dma((nspan,)),
            dma((2 * nz,)), dma((nz,)), dma((2 * nz,)), dma((2 * nz,)), dma((nz,)),
        ],
        compiler_params=pltpu.CompilerParams(
            collective_id=0, has_side_effects=True, vmem_limit_bytes=58 * 1024 * 1024
        ),
    )(
        noise_level, range_lo, range_len, hidden_in, mod_table,
        qkv_weight.transpose(1, 0, 2), out_weight,
    )


def solution(mesh):
    return jax.shard_map(
        functools.partial(local, mesh.shape["span"], mesh.shape["seq"]),
        mesh=mesh,
        in_specs=(
            P(("span", "seq"), None),
            P(None, None, "seq"),
            P("seq", None),
            P(),
            P(),
            P(),
            P(),
        ),
        out_specs=P(("span", "seq"), None),
        check_vma=False,
    )
```

```python
import functools

import jax
import jax.numpy as jnp
from jax import lax
from jax.experimental import pallas as pl
from jax.experimental.pallas import tpu as pltpu
from jax.sharding import PartitionSpec as P

HD = 128
F32 = jnp.float32
BF16 = jnp.bfloat16
MESH = pl.DeviceIdType.MESH


def kernel(
    nspan, nseq,
    level_ref, lo_ref, len_ref, x_ref, mod_ref, w_hbm, wo_hbm, out_ref,
    w, wo, xg, proj, keys_in, att, acc, mx, den, term, sib, from_low, from_high, fwd, total,
    w_sem, wo_sem,
    g_send_up, g_send_down, g_send_sib, g_recv_z, g_recv_sib,
    k_send, k_recv,
    s_send_z, s_send_sib, s_recv_low, s_recv_high, s_recv_sib,
):
    span = lax.axis_index("span")
    seq = lax.axis_index("seq")
    nz = nseq // 2
    z = seq // 2
    core = seq - 2 * z
    rows, width = x_ref.shape
    tok = rows * nseq
    chunk = 2 * rows
    wdev = w.shape[2]
    heads = wdev // HD
    up, down, other = seq + 2, seq - 2, 2 * z + 1 - core
    has_up, has_down = z < nz - 1, z > 0

    loads = [pltpu.make_async_copy(w_hbm.at[p], w.at[p], w_sem.at[p]) for p in range(3)]
    for p in (1, 2, 0):
        loads[p].start()
    load_out = pltpu.make_async_copy(wo_hbm, wo, wo_sem)
    load_out.start()

    barrier = pltpu.get_barrier_semaphore()

    @pl.when(has_up)
    def _():
        pl.semaphore_signal(barrier, inc=1, device_id=(span, up), device_id_type=MESH)

    @pl.when(has_down)
    def _():
        pl.semaphore_signal(barrier, inc=1, device_id=(span, down), device_id_type=MESH)

    pl.semaphore_signal(barrier, inc=1, device_id=(span, other), device_id_type=MESH)

    def greet(i, carry):
        pl.semaphore_signal(
            barrier, inc=1, device_id=(lax.rem(span + i, nspan), seq), device_id_type=MESH
        )
        return carry

    lax.fori_loop(1, nspan, greet, 0)

    def block(index):
        return pl.ds(pl.multiple_of(index * rows, rows), rows)

    def chunk_rows(index):
        return pl.ds(pl.multiple_of(index * chunk, chunk), chunk)

    x = x_ref[...].astype(F32)
    mod = mod_ref[level_ref[span]].astype(F32)
    mean = jnp.mean(x, axis=-1, keepdims=True)
    centred = x - mean
    var = jnp.mean(centred * centred, axis=-1, keepdims=True)
    normed = centred * lax.rsqrt(var + 1e-06) * (1.0 + mod[0:1]) + mod[1:2]
    xg[block(seq), :] = normed.astype(BF16)

    pl.semaphore_wait(
        barrier, has_up.astype(jnp.int32) + has_down.astype(jnp.int32) + nspan
    )

    def columns(part):
        return slice(part * (width // 2), (part + 1) * (width // 2))

    def g_copy(origin, part, target, send_sem, recv_sem):
        return pltpu.make_async_remote_copy(
            src_ref=xg.at[block(origin), columns(part)], dst_ref=xg.at[block(origin), columns(part)],
            send_sem=send_sem, recv_sem=recv_sem, device_id=(span, target), device_id_type=MESH,
        )

    def g_up(oz, part):
        at = 2 * oz + part
        return g_copy(2 * oz + core, part, up, g_send_up.at[at], g_recv_z.at[at])

    def g_down(oz, part):
        at = 2 * oz + part
        return g_copy(2 * oz + core, part, down, g_send_down.at[at], g_recv_z.at[at])

    def g_sib(oz, part):
        at = 2 * oz + part
        return g_copy(2 * oz + core, part, other, g_send_sib.at[at], g_recv_sib.at[at])

    def g_sib_in(oz, part):
        at = 2 * oz + part
        return g_copy(2 * oz + 1 - core, part, other, g_send_sib.at[at], g_recv_sib.at[at])

    def k_copy(i, oz):
        return pltpu.make_async_remote_copy(
            src_ref=proj.at[pl.ds(1, 2), chunk_rows(oz), :],
            dst_ref=keys_in.at[span, :, chunk_rows(oz), :],
            send_sem=k_send.at[i * nz + oz], recv_sem=k_recv.at[span * nz + oz],
            device_id=(i, seq), device_id_type=MESH,
        )

    def k_copy_in(i, oz):
        return pltpu.make_async_remote_copy(
            src_ref=proj.at[pl.ds(1, 2), chunk_rows(oz), :],
            dst_ref=keys_in.at[i, :, chunk_rows(oz), :],
            send_sem=k_send.at[i * nz + oz], recv_sem=k_recv.at[i * nz + oz],
            device_id=(i, seq), device_id_type=MESH,
        )

    def gather_step(k, carry):
        low, high = z - k, z + k

        for half_at in range(2):
            @pl.when((k > 0) & (low >= 0))
            def _():
                g_up(low, half_at).wait_recv()

            @pl.when((low >= 0) & has_up)
            def _():
                g_up(low, half_at).start()

            @pl.when((k > 0) & (high < nz))
            def _():
                g_down(high, half_at).wait_recv()

            @pl.when((high < nz) & has_down)
            def _():
                g_down(high, half_at).start()

            @pl.when(low >= 0)
            def _():
                g_sib(low, half_at).start()

            @pl.when((k > 0) & (high < nz))
            def _():
                g_sib(high, half_at).start()

        @pl.when(k == 0)
        def _():
            for p in range(3):
                loads[p].wait()

        def side(i, c):
            oz = jnp.where(i == 0, low, high)

            @pl.when(((i == 0) & (low >= 0)) | ((i == 1) & (k > 0) & (high < nz)))
            def _():
                g_sib_in(oz, 0).wait_recv()
                g_sib_in(oz, 1).wait_recv()

                def part(p, cc):
                    proj[p, chunk_rows(oz), :] = jnp.dot(
                        xg[chunk_rows(oz), :], w[p], preferred_element_type=F32
                    ).astype(BF16)
                    return cc

                lax.fori_loop(1, 3, part, 0)

                def send_keys(i, cc):
                    k_copy(i, oz).start()
                    return cc

                lax.fori_loop(span + 1, nspan, send_keys, 0)
                lax.fori_loop(0, 1, part, 0)

            return c

        lax.fori_loop(0, 2, side, 0)
        return carry

    lax.fori_loop(0, nz, gather_step, 0)

    scale = HD ** (-0.5)
    trans = (((1,), (1,)), ((), ()))
    for h in range(heads):
        cols = slice(h * HD, (h + 1) * HD)
        s = lax.dot_general(
            proj[0, :, cols], proj[1, :, cols], trans, preferred_element_type=F32
        ) * scale
        m = jnp.max(s, axis=-1, keepdims=True)
        e = jnp.exp(s - m)
        mx[h] = jnp.broadcast_to(m, (tok, HD))
        den[h] = jnp.broadcast_to(jnp.sum(e, axis=-1, keepdims=True), (tok, HD))
        acc[h] = jnp.dot(e.astype(BF16), proj[2, :, cols], preferred_element_type=F32)

    def await_window(j, carry):
        def one(oz, c):
            k_copy_in(j, oz).wait_recv()
            return c

        return lax.fori_loop(0, nz, one, carry)

    lax.fori_loop(0, span, await_window, 0)

    load_out.wait()

    def s_sib(d):
        return pltpu.make_async_remote_copy(
            src_ref=term.at[block(2 * d + 1 - core)], dst_ref=sib.at[d],
            send_sem=s_send_sib.at[d], recv_sem=s_recv_sib.at[d],
            device_id=(span, other), device_id_type=MESH,
        )

    def project(d):
        mine = chunk_rows(d)

        def see_window(j, carry):
            offset = lax.broadcasted_iota(jnp.int32, (chunk, tok), 1) - lo_ref[span, j]
            seen = (offset >= 0) & (offset < len_ref[span, j])
            for h in range(heads):
                cols = slice(h * HD, (h + 1) * HD)
                s = lax.dot_general(
                    proj[0, mine, cols], keys_in[j, 0, :, cols], trans,
                    preferred_element_type=F32,
                ) * scale
                s = jnp.where(seen, s, -1e30)
                old = mx[h, mine, :]
                new = jnp.maximum(old, jnp.max(s, axis=-1, keepdims=True))
                e = jnp.where(seen, jnp.exp(s - new[:, 0:1]), 0.0)
                factor = jnp.exp(old - new)
                mx[h, mine, :] = new
                den[h, mine, :] = den[h, mine, :] * factor + jnp.sum(e, axis=-1, keepdims=True)
                acc[h, mine, :] = acc[h, mine, :] * factor + jnp.dot(
                    e.astype(BF16), keys_in[j, 1, :, cols], preferred_element_type=F32
                )
            return carry

        lax.fori_loop(0, span, see_window, 0)
        for h in range(heads):
            att[mine, h * HD:(h + 1) * HD] = (acc[h, mine, :] / den[h, mine, :]).astype(BF16)
        term[mine, :] = jnp.dot(
            att[mine, :], wo[...], preferred_element_type=F32
        ).astype(BF16)
        s_sib(d).start()

    def s_up(d, part):
        return pltpu.make_async_remote_copy(
            src_ref=fwd.at[d, :, columns(part)], dst_ref=from_low.at[d, :, columns(part)],
            send_sem=s_send_z.at[2 * d + part], recv_sem=s_recv_low.at[2 * d + part],
            device_id=(span, up), device_id_type=MESH,
        )

    def s_down(d, part):
        return pltpu.make_async_remote_copy(
            src_ref=fwd.at[d, :, columns(part)], dst_ref=from_high.at[d, :, columns(part)],
            send_sem=s_send_z.at[2 * d + part], recv_sem=s_recv_high.at[2 * d + part],
            device_id=(span, down), device_id_type=MESH,
        )

    def pair(d, cols=slice(None)):
        return term[block(2 * d + core), cols].astype(F32) + sib[d, :, cols].astype(F32)

    def pass_on(d, copy, arrived, more):
        s_sib(d).wait_recv()
        for part in range(2):
            cols = columns(part)

            @pl.when(more)
            def _():
                copy(d, part).wait_recv()
                fwd[d, :, cols] = (pair(d, cols) + arrived[d, :, cols].astype(F32)).astype(BF16)

            @pl.when(jnp.logical_not(more))
            def _():
                fwd[d, :, cols] = pair(d, cols).astype(BF16)

            copy(d, part).start()

    def scatter_step(t):
        i = t - z
        d_up = nz - 1 - i

        @pl.when((i >= 0) & (d_up > z))
        def _():
            pass_on(d_up, s_up, from_low, has_down)

        d_down = t - (nz - 1 - z)

        @pl.when((d_down >= 0) & (d_down < z))
        def _():
            pass_on(d_down, s_down, from_high, has_up)

    at_end = jnp.logical_not(has_up & has_down)

    def step(u, carry):
        @pl.when(u < nz)
        def _():
            project(jnp.where(z >= nz // 2, u, nz - 1 - u))

        t = jnp.where(at_end, u, u - nz)

        @pl.when((t >= 0) & (t < nz - 1))
        def _():
            scatter_step(t)

        return carry

    lax.fori_loop(0, 2 * nz - 1, step, 0)

    s_sib(z).wait_recv()
    total[...] = x_ref[...].astype(F32) + pair(z)

    @pl.when(has_down)
    def _():
        s_up(z, 0).wait_recv()
        s_up(z, 1).wait_recv()
        total[...] += from_low[z].astype(F32)

    @pl.when(has_up)
    def _():
        s_down(z, 0).wait_recv()
        s_down(z, 1).wait_recv()
        total[...] += from_high[z].astype(F32)

    out_ref[...] = total[...].astype(BF16)

    def drain(oz, carry):
        s_sib(oz).wait_send()
        for part in range(2):
            g_sib(oz, part).wait_send()

            @pl.when((oz <= z) & has_up)
            def _():
                g_up(oz, part).wait_send()

            @pl.when((oz >= z) & has_down)
            def _():
                g_down(oz, part).wait_send()

            @pl.when(oz > z)
            def _():
                s_up(oz, part).wait_send()

            @pl.when(oz < z)
            def _():
                s_down(oz, part).wait_send()

        return carry

    lax.fori_loop(0, nz, drain, 0)

    def drain_window(i, carry):
        def one(oz, c):
            k_copy(i, oz).wait_send()
            return c

        return lax.fori_loop(0, nz, one, carry)

    lax.fori_loop(span + 1, nspan, drain_window, 0)


def local(nspan, nseq, hidden_in, qkv_weight, out_weight, mod_table, noise_level, range_lo, range_len):
    rows, width = hidden_in.shape
    wdev = qkv_weight.shape[2]
    tok = rows * nseq
    nz = nseq // 2
    heads = wdev // HD
    smem = pl.BlockSpec(memory_space=pltpu.SMEM)
    vmem = pl.BlockSpec(memory_space=pltpu.VMEM)
    hbm = pl.BlockSpec(memory_space=pl.ANY)
    dma = pltpu.SemaphoreType.DMA
    return pl.pallas_call(
        functools.partial(kernel, nspan, nseq),
        out_shape=jax.ShapeDtypeStruct((rows, width), BF16),
        in_specs=[smem, smem, smem, vmem, vmem, hbm, hbm],
        out_specs=vmem,
        scratch_shapes=[
            pltpu.VMEM((3, width, wdev), BF16),
            pltpu.VMEM((wdev, width), BF16),
            pltpu.VMEM((tok, width), BF16),
            pltpu.VMEM((3, tok, wdev), BF16),
            pltpu.VMEM((nspan, 2, tok, wdev), BF16),
            pltpu.VMEM((tok, wdev), BF16),
            pltpu.VMEM((heads, tok, HD), F32),
            pltpu.VMEM((heads, tok, HD), F32),
            pltpu.VMEM((heads, tok, HD), F32),
            pltpu.VMEM((tok, width), BF16),
            pltpu.VMEM((nz, rows, width), BF16),
            pltpu.VMEM((nz, rows, width), BF16),
            pltpu.VMEM((nz, rows, width), BF16),
            pltpu.VMEM((nz, rows, width), BF16),
            pltpu.VMEM((rows, width), F32),
            dma((3,)), dma(()),
            dma((2 * nz,)), dma((2 * nz,)), dma((2 * nz,)), dma((2 * nz,)), dma((2 * nz,)),
            dma((nspan * nz,)), dma((nspan * nz,)),
            dma((2 * nz,)), dma((nz,)), dma((2 * nz,)), dma((2 * nz,)), dma((nz,)),
        ],
        compiler_params=pltpu.CompilerParams(
            collective_id=0, has_side_effects=True, vmem_limit_bytes=58 * 1024 * 1024
        ),
    )(
        noise_level, range_lo, range_len, hidden_in, mod_table,
        qkv_weight.transpose(1, 0, 2), out_weight,
    )


def solution(mesh):
    return jax.shard_map(
        functools.partial(local, mesh.shape["span"], mesh.shape["seq"]),
        mesh=mesh,
        in_specs=(
            P(("span", "seq"), None),
            P(None, None, "seq"),
            P("seq", None),
            P(),
            P(),
            P(),
            P(),
        ),
        out_specs=P(("span", "seq"), None),
        check_vma=False,
    )
```
